128 devices in a mesh: section: 8 (over z_hi, y), tile: 16 (over x, z_lo, core).
Axes of the slice: x: 4, y: 4, z: 4 (z_hi: 2, z_lo: 2; z = z_hi * 2 + z_lo), core: 2. Of those that a mesh axis runs over, the one named last changes fastest.
Arguments:
- stored_inputs: bfloat16 [8, 4, 48, 128, 1024], P('section', None, 'tile'), may hold values from -6 to 6
- cotangent: bfloat16 [4, 48, 128, 1024], P(None, 'tile'), may hold values from -6 to 6
- w_reduce: bfloat16 [8, 1024, 256], P('section'), may hold values from -0.1875 to 0.1875
- w_spatial: bfloat16 [8, 2304, 256], P('section'), may hold values from -0.125 to 0.125
- w_expand: bfloat16 [8, 256, 1024], P('section'), may hold values from -0.375 to 0.375
- bias_reduce: float32 [8, 256], P('section'), may hold values from -1 to 1
- bias_spatial: float32 [8, 256], P('section'), may hold values from -1 to 1
- bias_expand: float32 [8, 1024], P('section'), may hold values from 0.5 to 2
Outputs:
- input_grads: bfloat16 [8, 4, 48, 128, 1024], P('section', None, 'tile')
- grad_reduce: float32 [8, 1024, 256], P('section', 'tile')
- grad_spatial: float32 [8, 2304, 256], P('section', 'tile')
- grad_expand: float32 [8, 256, 1024], P('section', 'tile')
The draws below stay inside these ranges and needn't reach their ends.
All inputs are finite; a program needn't handle non-finite values.
Results may differ from the reference program's by a relative error of at most 0.024.
Values may be sent and summed in bfloat16 or wider, within the bound.
No kernel may reach another device: no remote copies, remote signals or barrier semaphores. Data moves between devices by JAX's collectives and lax.ppermute only.
A program may use at most 64 MiB of HBM per device.

```python
import jax
import jax.numpy as jnp
from jax import lax

D = 1024
B = 256
COLS = 128
MICRO = 4
SECTIONS = 8
HEIGHT = 48


def block_scale(stream_key, shape, cuts, low, high):
    def one(position, blocks):
        draws = jax.random.uniform(jax.random.fold_in(jax.random.fold_in(stream_key, 6), position), (blocks,), jnp.float32, low / len(cuts), high / len(cuts))
        return jnp.repeat(jnp.exp(draws), shape[position] // blocks).reshape((-1,) + (1,) * (len(shape) - position - 1))

    gain = one(*cuts[0])
    for cut in cuts[1:]:
        gain = gain * one(*cut)
    return gain


def normal_values(key, extent, scale, bound, shards=(), dtype=jnp.bfloat16):
    gain = block_scale(key, extent, shards, -0.22, 0.18) if shards else 1.0
    array = jax.random.normal(key, extent, jnp.float32) * scale * gain
    return jnp.minimum(jnp.maximum(array, -bound), bound).astype(dtype)


def setup_inputs(seed: int = 0) -> dict:
    seeds = jax.random.split(jax.random.key(seed), 9)
    return {
        "stored_inputs": normal_values(seeds[0], (SECTIONS, MICRO, HEIGHT, COLS, D), 1.0, 6.0, ((0, 8), (2, 16))),
        "cotangent": normal_values(seeds[1], (MICRO, HEIGHT, COLS, D), 1.0, 6.0, ((1, 16),)),
        "w_reduce": normal_values(seeds[2], (SECTIONS, D, B), D ** -0.5, 0.1875, ((0, 8),)),
        "w_spatial": normal_values(seeds[3], (SECTIONS, 9 * B, B), (9 * B) ** -0.5, 0.125, ((0, 8),)),
        "w_expand": normal_values(seeds[4], (SECTIONS, B, D), B ** -0.5, 0.375, ((0, 8),)),
        "bias_reduce": jnp.clip(jax.random.uniform(seeds[5], (SECTIONS, B), jnp.float32, -1.0, 1.0) * block_scale(seeds[5], (SECTIONS, B), ((0, 8),), -0.4, 0.0), -1.0, 1.0),
        "bias_spatial": jnp.clip(jax.random.uniform(seeds[6], (SECTIONS, B), jnp.float32, -1.0, 1.0) * block_scale(seeds[6], (SECTIONS, B), ((0, 8),), -0.4, 0.0), -1.0, 1.0),
        "bias_expand": jnp.clip(0.5 + 1.5 * jax.random.uniform(seeds[7], (SECTIONS, D), jnp.float32) ** block_scale(seeds[7], (SECTIONS, D), ((0, 8),), -0.2, 0.2), 0.5, 2.0),
    }


def silu_slope(pre_act):
    sigma_val = jax.nn.sigmoid(pre_act)
    return sigma_val * (1.0 + pre_act * (1.0 - sigma_val))


def tap_views(padded, flip_sign):
    row_count = padded.shape[-3] - 2
    col_count = padded.shape[-2]
    widened = jnp.pad(padded, [(0, 0)] * (padded.ndim - 2) + [(1, 1), (0, 0)])
    pieces_list = []
    for row_off in (-1, 0, 1):
        for col_off in (-1, 0, 1):
            row_start = 1 + flip_sign * row_off
            col_start = 1 + flip_sign * col_off
            window = lax.slice_in_dim(widened, row_start, row_start + row_count, axis=widened.ndim - 3)
            window = lax.slice_in_dim(window, col_start, col_start + col_count, axis=widened.ndim - 2)
            pieces_list.append(window)
    return jnp.concatenate(pieces_list, axis=-1)


def contract_rows(left_mat, right_mat):
    return lax.dot_general(left_mat, right_mat, (((0,), (0,)), ((), ())), preferred_element_type=jnp.float32)


def contract_cols(left_mat, right_mat):
    return lax.dot_general(left_mat, right_mat, (((1,), (1,)), ((), ())), preferred_element_type=jnp.float32)


def reference(stored_inputs, cotangent, w_reduce, w_spatial, w_expand, bias_reduce, bias_spatial, bias_expand):
    section_count, micro_count, height, width_px, model_w = stored_inputs.shape
    bottle = w_reduce.shape[2]
    pixels = height * width_px
    sums_one = [jnp.zeros((model_w, bottle), jnp.float32) for section_id in range(section_count)]
    sums_two = [jnp.zeros((9 * bottle, bottle), jnp.float32) for section_id in range(section_count)]
    sums_three = [jnp.zeros((bottle, model_w), jnp.float32) for section_id in range(section_count)]
    results = [[None] * micro_count for section_id in range(section_count)]
    for micro_id in range(micro_count):
        upstream = cotangent[micro_id]
        for section_id in range(section_count - 1, -1, -1):
            flat_in = stored_inputs[section_id, micro_id].reshape(pixels, model_w)
            pre_one = jnp.dot(flat_in, w_reduce[section_id], preferred_element_type=jnp.float32) + bias_reduce[section_id]
            act_one = jax.nn.silu(pre_one).astype(jnp.bfloat16)
            padded = jnp.pad(act_one.reshape(height, width_px, bottle), ((1, 1), (0, 0), (0, 0)))
            patches = tap_views(padded, 1).reshape(pixels, 9 * bottle)
            pre_two = jnp.dot(patches, w_spatial[section_id], preferred_element_type=jnp.float32) + bias_spatial[section_id]
            act_two = jax.nn.silu(pre_two).astype(jnp.bfloat16)
            pre_three = jnp.dot(act_two, w_expand[section_id], preferred_element_type=jnp.float32) + bias_expand[section_id] + flat_in.astype(jnp.float32)
            slope_three = upstream.reshape(pixels, model_w).astype(jnp.float32) * silu_slope(pre_three)
            grad_three = slope_three.astype(jnp.bfloat16)
            sums_three[section_id] = sums_three[section_id] + contract_rows(act_two, grad_three)
            grad_two = (contract_cols(grad_three, w_expand[section_id]) * silu_slope(pre_two)).astype(jnp.bfloat16)
            sums_two[section_id] = sums_two[section_id] + contract_rows(patches, grad_two)
            grad_pad = jnp.pad(grad_two.reshape(height, width_px, bottle), ((1, 1), (0, 0), (0, 0)))
            back_patches = tap_views(grad_pad, -1).reshape(pixels, 9 * bottle)
            w_turned = w_spatial[section_id].reshape(9, bottle, bottle).transpose(0, 2, 1).reshape(9 * bottle, bottle)
            spatial_back = jnp.dot(back_patches, w_turned, preferred_element_type=jnp.float32)
            grad_one = (spatial_back * silu_slope(pre_one)).astype(jnp.bfloat16)
            sums_one[section_id] = sums_one[section_id] + contract_rows(flat_in, grad_one)
            input_grad = (contract_cols(grad_one, w_reduce[section_id]) + slope_three).astype(jnp.bfloat16)
            upstream = input_grad.reshape(height, width_px, model_w)
            results[section_id][micro_id] = upstream
    input_grads = jnp.stack([jnp.stack(results[section_id]) for section_id in range(section_count)])
    return input_grads, jnp.stack(sums_one), jnp.stack(sums_two), jnp.stack(sums_three)
```

```python
import jax
import jax.numpy as jnp
from jax import lax
from jax.experimental import pallas as pl
from jax.experimental.pallas import tpu as pltpu
from jax.sharding import PartitionSpec as P

F32 = jnp.float32
BF16 = jnp.bfloat16
NT = (((1,), (1,)), ((), ()))
TN = (((0,), (0,)), ((), ()))
MIB = 1024 * 1024


def silu_parts(v):
    s = 0.5 * jnp.tanh(0.5 * v) + 0.5
    return v * s, s * (1.0 + v * (1.0 - s))


def shifted(flat, width):
    n = flat.shape[0]
    col = lax.rem(lax.broadcasted_iota(jnp.int32, flat.shape, 0), width)
    left = jnp.where(col == 0, 0.0, pltpu.roll(flat, 1, 0))
    right = jnp.where(col == width - 1, 0.0, pltpu.roll(flat, n - 1, 0))
    return left, right


def spec(shape, index):
    return pl.BlockSpec(shape, index)


def fixed(shape):
    zeros = (0,) * len(shape)
    return pl.BlockSpec(shape, lambda *_: zeros)


def first_kernel(x_ref, w_ref, b_ref, act_ref, top_ref, bot_ref, s_ref, *, wide):
    _, rows, cols, dim = x_ref.shape
    pre = jnp.dot(x_ref[0].reshape(rows * cols, dim), w_ref[...], preferred_element_type=F32) + b_ref[...]
    act, slope = silu_parts(pre)
    act = act.reshape(rows, cols, -1).astype(BF16)
    act_ref[0] = act
    top_ref[0] = act[0]
    bot_ref[0] = act[rows - 1]
    slope = slope.reshape(rows, cols, -1)
    s_ref[0] = slope[:, :wide].astype(BF16)
    s_ref[1] = slope[:, cols - wide :].astype(BF16)


def second_kernel(
    flag_ref, act_ref, up_ref, dn_ref, x_ref, cot_ref, w2_ref, w3_ref, b2_ref, b3_ref,
    pcol_ref, act_two_ref, s_ref, d_ref, *, wide,
):
    _, rows, cols, dim = x_ref.shape
    mid = w3_ref.shape[0]
    pixels = rows * cols
    rims = jnp.concatenate(
        [up_ref[0].astype(F32), act_ref[0].astype(F32).reshape(pixels, mid), dn_ref[0].astype(F32)], axis=0
    )
    left, right = shifted(rims, cols)
    pcol = jnp.concatenate([left.astype(BF16), rims.astype(BF16), right.astype(BF16)], axis=1)
    pcol_ref[0] = pcol.reshape(rows + 2, cols, 3 * mid)
    pre = b2_ref[...]
    for dy in range(3):
        pre = pre + jnp.dot(
            pcol[dy * cols : dy * cols + pixels],
            w2_ref[dy * 3 * mid : (dy + 1) * 3 * mid],
            preferred_element_type=F32,
        )
    act, slope = silu_parts(pre)
    slope = slope.reshape(rows, cols, mid)
    s_ref[0] = slope[:, :wide].astype(BF16)
    s_ref[1] = slope[:, cols - wide :].astype(BF16)
    act_two = act.astype(BF16)
    act = act.reshape(rows, cols, mid)
    place = lax.broadcasted_iota(jnp.int32, (rows, wide, mid), 1)
    half = cols // 2
    act_two_ref[0] = jnp.where(place < half, act[:, :wide], 0.0).astype(BF16)
    act_two_ref[1] = jnp.where(place >= wide - half, act[:, cols - wide :], 0.0).astype(BF16)
    last = flag_ref[0] == 1
    for r in range(rows):
        pre = jnp.dot(act_two[r * cols : (r + 1) * cols], w3_ref[...], preferred_element_type=F32)
        pre = pre + b3_ref[...] + x_ref[0, r].astype(F32)
        slope = silu_parts(pre)[1]
        slope = slope * jnp.where(last, cot_ref[0, r].astype(F32), 1.0)
        d_ref[0, r] = slope[:wide].astype(BF16)
        d_ref[1, r] = slope[cols - wide :].astype(BF16)


def upper_kernel(
    idx_ref, v_ref, d_ref, s_ref, w3_ref, g3_in, g2_in,
    g3_ref, g2_all_ref, g2_ref, top_ref, bot_ref,
):
    rows, wide, dim = v_ref.shape
    half = g2_all_ref.shape[2]
    value = jnp.where(idx_ref[4] == 1, 1.0, v_ref[...].astype(F32))
    g3 = value * d_ref[0].astype(F32)
    g3_ref[0] = g3.astype(BF16)
    g3 = g3.reshape(rows * wide, dim).astype(BF16)
    g2 = lax.dot_general(g3, w3_ref[...], NT, preferred_element_type=F32)
    g2 = g2.reshape(rows, wide, -1) * s_ref[0].astype(F32)
    g2_ref[...] = g2.astype(BF16)
    top_ref[...] = g2[0].astype(BF16)
    bot_ref[...] = g2[rows - 1].astype(BF16)
    g2_all_ref[0] = jnp.where(idx_ref[3] == 0, g2[:, :half], g2[:, wide - half :]).astype(BF16)


def lower_kernel(
    idx_ref, g2_ref, up_ref, dn_ref, s_ref, g3_ref, w2_ref, w1_ref, g1_in, out_in,
    g1_all_ref, out_ref, v_ref,
):
    rows, wide, mid = g2_ref.shape
    dim = w1_ref.shape[0]
    half = out_ref.shape[2]
    n = rows * wide
    rims = jnp.concatenate(
        [up_ref[...].astype(F32), g2_ref[...].astype(F32).reshape(n, mid), dn_ref[...].astype(F32)], axis=0
    )
    left, right = shifted(rims, wide)
    views = (right, rims, left)
    back = None
    for dy in range(3):
        start = (2 - dy) * wide
        for dx in range(3):
            tap = 3 * dy + dx
            part = lax.dot_general(
                views[dx][start : start + n].astype(BF16),
                w2_ref[tap * mid : (tap + 1) * mid],
                NT,
                preferred_element_type=F32,
            )
            back = part if back is None else back + part
    g1 = back * s_ref[0].astype(F32).reshape(n, mid)
    g1_rows = g1.reshape(rows, wide, mid)
    low = idx_ref[3] == 0
    g1_all_ref[0] = jnp.where(low, g1_rows[:, :half], g1_rows[:, wide - half :]).astype(BF16)
    total = lax.dot_general(g1.astype(BF16), w1_ref[...], NT, preferred_element_type=F32)
    total = total.reshape(rows, wide, dim) + g3_ref[0].astype(F32)
    v_ref[...] = total.astype(BF16)
    out_ref[0] = jnp.where(low, total[:, :half], total[:, wide - half :]).astype(BF16)


def reduce_over_tiles(parts, x_size, z_size):
    me = lax.axis_index("tile")
    core, z, x = me % 2, (me // 2) % z_size, me // (2 * z_size)
    count = 2 * x_size * z_size
    sends = lax.dynamic_index_in_dim(parts, 1 - core, 2, keepdims=False)
    keeps = lax.dynamic_index_in_dim(parts, core, 2, keepdims=False)
    came = lax.ppermute(sends, "tile", [(i, i ^ 1) for i in range(count)])
    both = (keeps.astype(F32) + came.astype(F32)).astype(BF16)

    def at(dx, dz):
        row = lax.dynamic_index_in_dim(both, (x + dx) % x_size, 0, keepdims=False)
        return lax.dynamic_index_in_dim(row, (z + dz) % z_size, 0, keepdims=False)

    def target(i, dx, dz):
        ic, iz, ix = i % 2, (i // 2) % z_size, i // (2 * z_size)
        return (((ix + dx) % x_size) * z_size + (iz + dz) % z_size) * 2 + ic

    total = at(0, 0).astype(F32)
    for dz in range(z_size - 1, -1, -1):
        for dx in sorted(range(x_size), key=lambda d: -min(d, x_size - d)):
            if dx or dz:
                got = lax.ppermute(at(dx, dz), "tile", [(i, target(i, dx, dz)) for i in range(count)])
                total = total + got.astype(F32)
    return total


def local(
    stored_inputs, cotangent, w_reduce, w_spatial, w_expand, bias_reduce, bias_spatial, bias_expand
):
    x_all = stored_inputs[0]
    micros, rows, cols, dim = x_all.shape
    w1, w2, w3 = w_reduce[0], w_spatial[0], w_expand[0]
    mid = w1.shape[1]
    sections, tiles = lax.axis_size("section"), lax.axis_size("tile")
    me = lax.axis_index("section")
    half = cols // 2
    wide = half + sections
    chunks = 2 * micros
    both = ("section", "tile")

    def halo(top, bot, live):
        up_pairs, dn_pairs = [], []
        for s in live:
            for t in range(tiles - 1):
                up_pairs.append((s * tiles + t, s * tiles + t + 1))
                dn_pairs.append((s * tiles + t + 1, s * tiles + t))
        return lax.ppermute(bot, both, up_pairs), lax.ppermute(top, both, dn_pairs)

    params = pltpu.CompilerParams(vmem_limit_bytes=40 * MIB)
    act, top, bot, s1 = pl.pallas_call(
        lambda *refs: first_kernel(*refs, wide=wide),
        grid=(micros,),
        in_specs=[
            spec((1, rows, cols, dim), lambda m: (m, 0, 0, 0)),
            fixed((dim, mid)),
            fixed((1, mid)),
        ],
        out_specs=[
            spec((1, rows, cols, mid), lambda m: (m, 0, 0, 0)),
            spec((1, cols, mid), lambda m: (m, 0, 0)),
            spec((1, cols, mid), lambda m: (m, 0, 0)),
            spec((2, rows, wide, mid), lambda m: (m, 0, 0, 0)),
        ],
        out_shape=[
            jax.ShapeDtypeStruct((micros, rows, cols, mid), BF16),
            jax.ShapeDtypeStruct((micros, cols, mid), BF16),
            jax.ShapeDtypeStruct((micros, cols, mid), BF16),
            jax.ShapeDtypeStruct((chunks, rows, wide, mid), BF16),
        ],
        compiler_params=params,
        name="first",
    )(x_all, w1, bias_reduce)
    up, dn = halo(top, bot, range(sections))
    is_last = (me == sections - 1).astype(jnp.int32)
    pcol, act_two, s2, d3 = pl.pallas_call(
        lambda *refs: second_kernel(*refs, wide=wide),
        grid=(micros,),
        in_specs=[
            pl.BlockSpec(memory_space=pltpu.SMEM),
            spec((1, rows, cols, mid), lambda m: (m, 0, 0, 0)),
            spec((1, cols, mid), lambda m: (m, 0, 0)),
            spec((1, cols, mid), lambda m: (m, 0, 0)),
            spec((1, rows, cols, dim), lambda m: (m, 0, 0, 0)),
            spec((1, rows, cols, dim), lambda m: (m, 0, 0, 0)),
            fixed((9 * mid, mid)),
            fixed((mid, dim)),
            fixed((1, mid)),
            fixed((1, dim)),
        ],
        out_specs=[
            spec((1, rows + 2, cols, 3 * mid), lambda m: (m, 0, 0, 0)),
            spec((2, rows, wide, mid), lambda m: (m, 0, 0, 0)),
            spec((2, rows, wide, mid), lambda m: (m, 0, 0, 0)),
            spec((2, rows, wide, dim), lambda m: (m, 0, 0, 0)),
        ],
        out_shape=[
            jax.ShapeDtypeStruct((micros, rows + 2, cols, 3 * mid), BF16),
            jax.ShapeDtypeStruct((chunks, rows, wide, mid), BF16),
            jax.ShapeDtypeStruct((chunks, rows, wide, mid), BF16),
            jax.ShapeDtypeStruct((chunks, rows, wide, dim), BF16),
        ],
        compiler_params=params,
        name="second",
    )(is_last[None], act, up, dn, x_all, cotangent, w2, w3, bias_spatial, bias_expand)

    g3_all = jnp.zeros((chunks + 1, rows, wide, dim), BF16)
    g2_all = jnp.zeros((micros + 1, rows, cols, mid), BF16)
    g1_all = jnp.zeros((micros + 1, rows, cols, mid), BF16)
    out_all = jnp.zeros((micros + 1, rows, cols, dim), BF16)
    value = jnp.zeros((rows, wide, dim), BF16)

    upper = pl.pallas_call(
        upper_kernel,
        grid_spec=pltpu.PrefetchScalarGridSpec(
            num_scalar_prefetch=1,
            grid=(1,),
            in_specs=[
                fixed((rows, wide, dim)),
                spec((1, rows, wide, dim), lambda _, i: (i[0], 0, 0, 0)),
                spec((1, rows, wide, mid), lambda _, i: (i[0], 0, 0, 0)),
                fixed((mid, dim)),
                pl.BlockSpec(memory_space=pl.ANY),
                pl.BlockSpec(memory_space=pl.ANY),
            ],
            out_specs=[
                spec((1, rows, wide, dim), lambda _, i: (i[1], 0, 0, 0)),
                spec((1, rows, half, mid), lambda _, i: (i[2], 0, i[3], 0)),
                fixed((rows, wide, mid)),
                fixed((wide, mid)),
                fixed((wide, mid)),
            ],
        ),
        out_shape=[
            jax.ShapeDtypeStruct(g3_all.shape, BF16),
            jax.ShapeDtypeStruct(g2_all.shape, BF16),
            jax.ShapeDtypeStruct((rows, wide, mid), BF16),
            jax.ShapeDtypeStruct((wide, mid), BF16),
            jax.ShapeDtypeStruct((wide, mid), BF16),
        ],
        input_output_aliases={5: 0, 6: 1},
        compiler_params=params,
        name="upper",
    )
    lower = pl.pallas_call(
        lower_kernel,
        grid_spec=pltpu.PrefetchScalarGridSpec(
            num_scalar_prefetch=1,
            grid=(1,),
            in_specs=[
                fixed((rows, wide, mid)),
                fixed((wide, mid)),
                fixed((wide, mid)),
                spec((1, rows, wide, mid), lambda _, i: (i[0], 0, 0, 0)),
                spec((1, rows, wide, dim), lambda _, i: (i[1], 0, 0, 0)),
                fixed((9 * mid, mid)),
                fixed((dim, mid)),
                pl.BlockSpec(memory_space=pl.ANY),
                pl.BlockSpec(memory_space=pl.ANY),
            ],
            out_specs=[
                spec((1, rows, half, mid), lambda _, i: (i[2], 0, i[3], 0)),
                spec((1, rows, half, dim), lambda _, i: (i[2], 0, i[3], 0)),
                fixed((rows, wide, dim)),
            ],
        ),
        out_shape=[
            jax.ShapeDtypeStruct(g1_all.shape, BF16),
            jax.ShapeDtypeStruct(out_all.shape, BF16),
            jax.ShapeDtypeStruct((rows, wide, dim), BF16),
        ],
        input_output_aliases={8: 0, 9: 1},
        compiler_params=params,
        name="lower",
    )

    for step in range(chunks + sections - 1):
        raw = step - (sections - 1 - me)
        live = (raw >= 0) & (raw < chunks)
        chunk = jnp.clip(raw, 0, chunks - 1)
        idx = jnp.stack([
            chunk,
            jnp.where(live, chunk, chunks),
            jnp.where(live, chunk // 2, micros),
            chunk % 2,
            is_last,
        ]).astype(jnp.int32)
        alive = [s for s in range(sections) if 0 <= step - (sections - 1 - s) < chunks]
        g3_all, g2_all, g2, top, bot = upper(idx, value, d3, s2, w3, g3_all, g2_all)
        up, dn = halo(top, bot, alive)
        g1_all, out_all, value = lower(idx, g2, up, dn, s1, g3_all, w2, w1, g1_all, out_all)
        if step < chunks + sections - 2:
            value = lax.ppermute(value, "section", [(s, s - 1) for s in alive if s > 0])

    pixels = micros * rows * cols
    g1 = g1_all[:micros].reshape(pixels, mid)
    g2 = g2_all[:micros].reshape(pixels, mid)

    def dot_rows(left, right):
        return lax.dot_general(left, right, TN, preferred_element_type=F32).astype(BF16)

    sum_three = dot_rows(
        act_two.reshape(chunks * rows * wide, mid), g3_all[:chunks].reshape(chunks * rows * wide, dim)
    )
    sum_two = jnp.concatenate(
        [dot_rows(pcol[:, dy : dy + rows].reshape(pixels, 3 * mid), g2) for dy in range(3)], axis=0
    )
    sum_one = dot_rows(x_all.reshape(pixels, dim), g1)
    sizes = [dim * mid // tiles, 9 * mid * mid // tiles, mid * dim // tiles]
    x_size, z_size = 4, 2
    parts = jnp.concatenate(
        [v.reshape(tiles, n // 256, 256) for v, n in zip((sum_one, sum_two, sum_three), sizes)], axis=1
    ).reshape(x_size, z_size, 2, sum(sizes) // 256, 256)
    total = reduce_over_tiles(parts, x_size, z_size)
    cut = [0, sizes[0] // 256, (sizes[0] + sizes[1]) // 256, sum(sizes) // 256]
    one = total[cut[0] : cut[1]].reshape(1, dim // tiles, mid)
    two = total[cut[1] : cut[2]].reshape(1, 9 * mid // tiles, mid)
    three = total[cut[2] : cut[3]].reshape(1, mid // tiles, dim)
    return (out_all[:micros][None], one, two, three)


def solution(mesh):
    return jax.shard_map(
        local,
        mesh=mesh,
        in_specs=(
            P("section", None, "tile", None, None),
            P(None, "tile", None, None),
            P("section", None, None),
            P("section", None, None),
            P("section", None, None),
            P("section", None),
            P("section", None),
            P("section", None),
        ),
        out_specs=(
            P("section", None, "tile", None, None),
            P("section", "tile", None),
            P("section", "tile", None),
            P("section", "tile", None),
        ),
        check_vma=False,
    )
```

```python
import jax
import jax.numpy as jnp
from jax import lax
from jax.experimental import pallas as pl
from jax.experimental.pallas import tpu as pltpu
from jax.sharding import PartitionSpec as P

F32 = jnp.float32
BF16 = jnp.bfloat16
NT = (((1,), (1,)), ((), ()))
TN = (((0,), (0,)), ((), ()))
MIB = 1024 * 1024
BIG, SMALL = 24, 16


def silu_parts(v):
    s = 0.5 * jnp.tanh(0.5 * v) + 0.5
    return v * s, s * (1.0 + v * (1.0 - s))


def shifted(flat, width):
    n = flat.shape[0]
    col = lax.rem(lax.broadcasted_iota(jnp.int32, flat.shape, 0), width)
    left = jnp.where(col == 0, 0.0, pltpu.roll(flat, 1, 0))
    right = jnp.where(col == width - 1, 0.0, pltpu.roll(flat, n - 1, 0))
    return left, right


def spec(shape, index):
    return pl.BlockSpec(shape, index)


def fixed(shape):
    zeros = (0,) * len(shape)
    return pl.BlockSpec(shape, lambda *_: zeros)


def first_kernel(*refs, wide):
    base_ref, x_ref, w_ref, b_ref = refs[:4]
    act_ref, even_ref, odd_ref, s_ref = refs[-4:]
    _, rows, cols, dim = x_ref.shape
    pre = jnp.dot(x_ref[0].reshape(rows * cols, dim), w_ref[...], preferred_element_type=F32) + b_ref[...]
    act, slope = silu_parts(pre)
    act = act.reshape(rows, cols, -1)
    act_ref[0] = act.astype(BF16)
    odd = base_ref[4] == 1
    even_ref[0] = jnp.where(odd, act[0], act[rows - 1]).astype(BF16)
    odd_ref[0] = jnp.where(odd, act[rows - 1], act[0]).astype(BF16)
    slope = slope.reshape(rows, cols, -1)
    s_ref[0] = slope[:, :wide].astype(BF16)
    s_ref[1] = slope[:, cols - wide :].astype(BF16)


def second_kernel(*refs, wide):
    base_ref, act_ref, even_ref, odd_ref, x_ref, cot_ref, w2_ref, w3_ref, b2_ref, b3_ref = refs[:10]
    pcol_ref, act_two_ref, s_ref, d_ref = refs[-4:]
    _, rows, cols, dim = x_ref.shape
    mid = w3_ref.shape[0]
    pixels = rows * cols
    up, dn = edge_rows(base_ref, even_ref[0].astype(F32), odd_ref[0].astype(F32))
    rims = jnp.concatenate([up, act_ref[0].astype(F32).reshape(pixels, mid), dn], axis=0)
    left, right = shifted(rims, cols)
    pcol = jnp.concatenate([left.astype(BF16), rims.astype(BF16), right.astype(BF16)], axis=1)
    pcol_ref[0] = pcol.reshape(rows + 2, cols, 3 * mid)
    pre = b2_ref[...]
    for dy in range(3):
        pre = pre + jnp.dot(
            pcol[dy * cols : dy * cols + pixels],
            w2_ref[dy * 3 * mid : (dy + 1) * 3 * mid],
            preferred_element_type=F32,
        )
    act, slope = silu_parts(pre)
    slope = slope.reshape(rows, cols, mid)
    s_ref[0] = slope[:, :wide].astype(BF16)
    s_ref[1] = slope[:, cols - wide :].astype(BF16)
    act_two = act.astype(BF16)
    act_two_ref[0] = act.reshape(rows, cols, mid).astype(BF16)
    last = base_ref[1] == 1
    for r in range(rows):
        pre = jnp.dot(act_two[r * cols : (r + 1) * cols], w3_ref[...], preferred_element_type=F32)
        pre = pre + b3_ref[...] + x_ref[0, r].astype(F32)
        slope = silu_parts(pre)[1]
        slope = slope * jnp.where(last, cot_ref[0, r].astype(F32), 1.0)
        d_ref[0, r] = slope[:wide].astype(BF16)
        d_ref[1, r] = slope[cols - wide :].astype(BF16)


def start_if(cond, *copies):
    @pl.when(cond)
    def _():
        for copy in copies:
            copy.start()


def wait_if(cond, *copies):
    @pl.when(cond)
    def _():
        for copy in copies:
            copy.wait()


def place_of(step, base_ref, chunks):
    raw = step - base_ref[0]
    return jnp.clip(raw, 0, chunks - 1), jnp.logical_and(raw >= 0, raw < chunks)


def piece_of(array, chunk, half):
    where = pl.ds(pl.multiple_of(lax.rem(chunk, 2) * half, half), half)
    return array.at[lax.div(chunk, 2), :, where]


def upper_kernel(*refs, step, chunks, late):
    base_ref, early_ref, refs = refs[0], refs[1], refs[2:]
    if late:
        late_ref, refs = refs[0], refs[1:]
    d_ref, s2_ref, s1_ref, w3_ref, out_piece, _ = refs[:6]
    out_all, g3_ref, g2_ref, even_ref, odd_ref, g3_piece, g2_piece, s1_out, sems = refs[6:]
    rows, wide, dim = d_ref.shape
    half = g2_piece.shape[1]
    chunk, _ = place_of(step, base_ref, chunks)
    get_s = pltpu.make_async_copy(s1_ref.at[chunk], s1_out, sems.at[0])
    get_s.start()
    before, had = place_of(step - 1, base_ref, chunks)
    if step:
        put = pltpu.make_async_copy(out_piece, piece_of(out_all, before, half), sems.at[1])
        start_if(had, put)
    value = early_ref[...].astype(F32)
    if late:
        value = jnp.where(base_ref[5] == 1, late_ref[...].astype(F32), value)
    value = jnp.where(base_ref[1] == 1, 1.0, value)
    g3 = value * d_ref[...].astype(F32)
    g3_ref[...] = g3.astype(BF16)
    low = lax.rem(chunk, 2) == 0
    g3_piece[...] = jnp.where(low, g3[:, :half], g3[:, wide - half :]).astype(BF16)
    g3 = g3.reshape(rows * wide, dim).astype(BF16)
    g2 = lax.dot_general(g3, w3_ref[...], NT, preferred_element_type=F32)
    g2 = g2.reshape(rows, wide, -1) * s2_ref[...].astype(F32)
    g2_ref[...] = g2.astype(BF16)
    odd = base_ref[4] == 1
    even_ref[...] = jnp.where(odd, g2[0], g2[rows - 1]).astype(BF16)
    odd_ref[...] = jnp.where(odd, g2[rows - 1], g2[0]).astype(BF16)
    g2_piece[...] = jnp.where(low, g2[:, :half], g2[:, wide - half :]).astype(BF16)
    if step:
        wait_if(had, put)
    get_s.wait()


def lower_kernel(
    base_ref, g2_ref, even_ref, odd_ref, s1_ref, g3_ref, w2_ref, w1_ref, d_ref, s2_ref, after_ref,
    v_ref, out_piece, g1_piece, d_out, s2_out, sems, *, step,
):
    rows, wide, mid = g2_ref.shape
    dim = w1_ref.shape[0]
    half = out_piece.shape[1]
    n = rows * wide
    chunks = d_ref.shape[0]
    chunk, _ = place_of(step, base_ref, chunks)
    later, _ = place_of(step + 1, base_ref, chunks)
    get_d = pltpu.make_async_copy(d_ref.at[later], d_out, sems.at[0])
    get_s = pltpu.make_async_copy(s2_ref.at[later], s2_out, sems.at[1])
    get_d.start()
    get_s.start()
    up, dn = edge_rows(base_ref, even_ref[...].astype(F32), odd_ref[...].astype(F32))
    rims = jnp.concatenate([up, g2_ref[...].astype(F32).reshape(n, mid), dn], axis=0)
    left, right = shifted(rims, wide)
    views = (right, rims, left)
    back = None
    for dy in range(3):
        start = (2 - dy) * wide
        for dx in range(3):
            tap = 3 * dy + dx
            part = lax.dot_general(
                views[dx][start : start + n].astype(BF16),
                w2_ref[tap * mid : (tap + 1) * mid],
                NT,
                preferred_element_type=F32,
            )
            back = part if back is None else back + part
    g1 = back * s1_ref[...].astype(F32).reshape(n, mid)
    g1_rows = g1.reshape(rows, wide, mid)
    low = lax.rem(chunk, 2) == 0
    g1_piece[...] = jnp.where(low, g1_rows[:, :half], g1_rows[:, wide - half :]).astype(BF16)
    total = lax.dot_general(g1.astype(BF16), w1_ref[...], NT, preferred_element_type=F32)
    total = total.reshape(rows, wide, dim) + g3_ref[...].astype(F32)
    v_ref[...] = total.astype(BF16)
    out_piece[...] = jnp.where(low, total[:, :half], total[:, wide - half :]).astype(BF16)
    get_d.wait()
    get_s.wait()


def flush_kernel(base_ref, out_piece, out_in, out_all, sem, *, step, chunks):
    chunk, live = place_of(step, base_ref, chunks)
    put = pltpu.make_async_copy(out_piece, piece_of(out_all, chunk, out_piece.shape[1]), sem)
    start_if(live, put)
    wait_if(live, put)


def weights_kernel(*refs, step, chunks):
    base_ref, x_ref, pcol_ref, act_ref, g3_ref, g2_ref, g1_ref, _ = refs[:8]
    olds, (one, two, three, x_buf, p_buf, a_buf, sems) = refs[8:-7], refs[-7:]
    rows, half, dim = x_buf.shape
    mid = a_buf.shape[2]
    chunk, live = place_of(step, base_ref, chunks)
    gets = [
        pltpu.make_async_copy(piece_of(src, chunk, half), dst, sems.at[i])
        for i, (src, dst) in enumerate(((x_ref, x_buf), (pcol_ref, p_buf), (act_ref, a_buf)))
    ]
    start_if(live, *gets)
    pixels = rows * half

    def put(ref, old, place, term):
        ref[place] = term if old is None else old[place] + term

    old_one, old_two, old_three = olds if olds else (None, None, None)

    @pl.when(live)
    def _():
        for get in gets:
            get.wait()
        g3 = g3_ref[...].reshape(pixels, dim)
        g2 = g2_ref[...].reshape(pixels, mid)
        g1 = g1_ref[...].reshape(pixels, mid)
        all_rows = slice(None)
        put(three, old_three, all_rows, lax.dot_general(
            a_buf[...].reshape(pixels, mid), g3, TN, preferred_element_type=F32))
        put(one, old_one, all_rows, lax.dot_general(
            x_buf[...].reshape(pixels, dim), g1, TN, preferred_element_type=F32))
        for dy in range(3):
            put(two, old_two, slice(dy * 3 * mid, (dy + 1) * 3 * mid), lax.dot_general(
                p_buf[dy : dy + rows].reshape(pixels, 3 * mid), g2, TN, preferred_element_type=F32))

    @pl.when(jnp.logical_not(live))
    def _():
        for ref, old in ((one, old_one), (two, old_two), (three, old_three)):
            ref[...] = jnp.zeros_like(ref) if old is None else old[...]


def edge_rows(base_ref, even, odd):
    flip = base_ref[4] == 1
    up = jnp.where(base_ref[2] == 1, jnp.where(flip, even, odd), 0.0)
    dn = jnp.where(base_ref[3] == 1, jnp.where(flip, odd, even), 0.0)
    return up, dn


def reduce_over_tiles(parts, x_size, z_size):
    me = lax.axis_index("tile")
    core, z, x = me % 2, (me // 2) % z_size, me // (2 * z_size)
    count = 2 * x_size * z_size
    sends = lax.dynamic_index_in_dim(parts, 1 - core, 2, keepdims=False)
    keeps = lax.dynamic_index_in_dim(parts, core, 2, keepdims=False)
    came = lax.ppermute(sends, "tile", [(i, i ^ 1) for i in range(count)])
    both = (keeps.astype(F32) + came.astype(F32)).astype(BF16)

    def at(dx, dz):
        row = lax.dynamic_index_in_dim(both, (x + dx) % x_size, 0, keepdims=False)
        return lax.dynamic_index_in_dim(row, (z + dz) % z_size, 0, keepdims=False)

    def target(i, dx, dz):
        ic, iz, ix = i % 2, (i // 2) % z_size, i // (2 * z_size)
        return (((ix + dx) % x_size) * z_size + (iz + dz) % z_size) * 2 + ic

    total = at(0, 0).astype(F32)
    for dz in range(z_size - 1, -1, -1):
        for dx in sorted(range(x_size), key=lambda d: -min(d, x_size - d)):
            if dx or dz:
                got = lax.ppermute(at(dx, dz), "tile", [(i, target(i, dx, dz)) for i in range(count)])
                total = total + got.astype(F32)
    return total


def local(
    stored_inputs, cotangent, w_reduce, w_spatial, w_expand, bias_reduce, bias_spatial, bias_expand
):
    x_all = stored_inputs[0]
    micros, rows, cols, dim = x_all.shape
    w1, w2, w3 = w_reduce[0], w_spatial[0], w_expand[0]
    mid = w1.shape[1]
    sections, tiles = lax.axis_size("section"), lax.axis_size("tile")
    me, tile = lax.axis_index("section"), lax.axis_index("tile")
    half = cols // 2
    wide = half + sections
    chunks = 2 * micros
    cross = sections // 2
    base = jnp.stack([
        2 * (sections - 1 - me) + (me < cross),
        me == sections - 1,
        tile > 0,
        tile < tiles - 1,
        tile % 2,
        me == cross - 1,
    ]).astype(jnp.int32)
    pairs_even = [(t, t ^ 1) for t in range(tiles)]
    ends = (0, tiles - 1)
    pairs_odd = [(t, t if t in ends else t + 1 if t % 2 else t - 1) for t in range(tiles)]
    pairs_z = [(t, t ^ 2) for t in range(tiles)]
    pairs_down = [
        (s * tiles + t, (s - 1) % sections * tiles + (t if s % cross else t ^ 2))
        for s in range(sections)
        for t in range(tiles)
    ]

    def exchange(even, odd):
        return lax.ppermute(even, "tile", pairs_even), lax.ppermute(odd, "tile", pairs_odd)

    big = pltpu.CompilerParams(vmem_limit_bytes=BIG * MIB)
    small = pltpu.CompilerParams(vmem_limit_bytes=SMALL * MIB)
    smem = pl.BlockSpec(memory_space=pltpu.SMEM)
    vmem = pl.BlockSpec(memory_space=pltpu.VMEM)
    hbm = pl.BlockSpec(memory_space=pltpu.HBM)
    anywhere = pl.BlockSpec(memory_space=pl.ANY)

    def like(*shape):
        return jax.ShapeDtypeStruct(shape, BF16)

    def first(begin, end, s_in):
        extra = [] if s_in is None else [s_in]
        count = end - begin
        return pl.pallas_call(
            lambda *refs: first_kernel(*refs, wide=wide),
            grid=(count,),
            in_specs=[
                smem,
                spec((1, rows, cols, dim), lambda m: (m + begin, 0, 0, 0)),
                fixed((dim, mid)),
                fixed((1, mid)),
            ] + [hbm] * len(extra),
            out_specs=[
                spec((1, rows, cols, mid), lambda m: (m, 0, 0, 0)),
                spec((1, cols, mid), lambda m: (m, 0, 0)),
                spec((1, cols, mid), lambda m: (m, 0, 0)),
                spec((2, rows, wide, mid), lambda m: (m + begin, 0, 0, 0)),
            ],
            out_shape=[
                like(count, rows, cols, mid),
                like(count, cols, mid),
                like(count, cols, mid),
                like(chunks, rows, wide, mid),
            ],
            input_output_aliases={4: 3} if extra else {},
            compiler_params=big,
            name="first",
        )(base, x_all, w1, bias_reduce, *extra)

    def second(micro, at, act, even, odd, earlier, after):
        extra = [] if earlier is None else [*earlier, after]
        return pl.pallas_call(
            lambda *refs: second_kernel(*refs, wide=wide),
            grid=(1,),
            in_specs=[
                smem,
                spec((1, rows, cols, mid), lambda m: (at, 0, 0, 0)),
                spec((1, cols, mid), lambda m: (at, 0, 0)),
                spec((1, cols, mid), lambda m: (at, 0, 0)),
                spec((1, rows, cols, dim), lambda m: (micro, 0, 0, 0)),
                spec((1, rows, cols, dim), lambda m: (micro, 0, 0, 0)),
                fixed((9 * mid, mid)),
                fixed((mid, dim)),
                fixed((1, mid)),
                fixed((1, dim)),
            ] + ([hbm] * 4 + [anywhere] if extra else []),
            out_specs=[
                spec((1, rows + 2, cols, 3 * mid), lambda m: (micro, 0, 0, 0)),
                spec((1, rows, cols, mid), lambda m: (micro, 0, 0, 0)),
                spec((2, rows, wide, mid), lambda m: (micro, 0, 0, 0)),
                spec((2, rows, wide, dim), lambda m: (micro, 0, 0, 0)),
            ],
            out_shape=[
                like(micros, rows + 2, cols, 3 * mid),
                like(micros, rows, cols, mid),
                like(chunks, rows, wide, mid),
                like(chunks, rows, wide, dim),
            ],
            input_output_aliases={10: 0, 11: 1, 12: 2, 13: 3} if extra else {},
            compiler_params=big,
            name="second",
        )(base, act, even, odd, x_all, cotangent, w2, w3, bias_spatial, bias_expand, *extra)

    def upper(step, early, late):
        values = [early] if late is None else [early, late]
        k = len(values)
        return pl.pallas_call(
            lambda *refs: upper_kernel(*refs, step=step, chunks=chunks, late=late is not None),
            in_specs=[smem] + [vmem] * k + [vmem, vmem, hbm, vmem, vmem, hbm],
            out_specs=[hbm] + [vmem] * 7,
            out_shape=[
                like(*out_all.shape),
                like(rows, wide, dim),
                like(rows, wide, mid),
                like(wide, mid),
                like(wide, mid),
                like(rows, half, dim),
                like(rows, half, mid),
                like(rows, wide, mid),
            ],
            scratch_shapes=[pltpu.SemaphoreType.DMA((2,))],
            input_output_aliases={6 + k: 0},
            compiler_params=small,
            name="upper",
        )(base, *values, d_now, s2_now, s1, w3, out_piece, out_all)

    def lower(step, g2, even, odd, g3, s1_now, after):
        return pl.pallas_call(
            lambda *refs: lower_kernel(*refs, step=step),
            in_specs=[smem] + [vmem] * 7 + [hbm] * 2 + [anywhere],
            out_specs=[vmem] * 5,
            out_shape=[
                like(rows, wide, dim),
                like(rows, half, dim),
                like(rows, half, mid),
                like(rows, wide, dim),
                like(rows, wide, mid),
            ],
            scratch_shapes=[pltpu.SemaphoreType.DMA((2,))],
            compiler_params=small,
            name="lower",
        )(base, g2, even, odd, s1_now, g3, w2, w1, d3, s2, after)

    def flush(step):
        return pl.pallas_call(
            lambda *refs: flush_kernel(*refs, step=step, chunks=chunks),
            in_specs=[smem, vmem, hbm],
            out_specs=hbm,
            out_shape=like(*out_all.shape),
            scratch_shapes=[pltpu.SemaphoreType.DMA],
            input_output_aliases={2: 0},
            compiler_params=small,
            name="flush",
        )(base, out_piece, out_all)

    def weights(step, g3, g2, g1, after, olds):
        shapes = [(dim, mid), (9 * mid, mid), (mid, dim)]
        return pl.pallas_call(
            lambda *refs: weights_kernel(*refs, step=step, chunks=chunks),
            in_specs=[smem, hbm, hbm, hbm, vmem, vmem, vmem, anywhere] + [vmem] * len(olds),
            out_specs=[vmem] * 3,
            out_shape=[jax.ShapeDtypeStruct(shape, F32) for shape in shapes],
            scratch_shapes=[
                pltpu.VMEM((rows, half, dim), BF16),
                pltpu.VMEM((rows + 2, half, 3 * mid), BF16),
                pltpu.VMEM((rows, half, mid), BF16),
                pltpu.SemaphoreType.DMA((3,)),
            ],
            input_output_aliases={8: 0, 9: 1, 10: 2} if olds else {},
            compiler_params=small,
            name="weights",
        )(base, x_all, pcol, act_two, g3, g2, g1, after, *olds)

    act_a, even, odd, s1 = first(0, 1, None)
    even_a, odd_a = exchange(even, odd)
    act_b, even, odd, s1 = first(1, micros, s1)
    even_b, odd_b = exchange(even, odd)
    forward = second(0, 0, act_a, even_a, odd_a, None, None)

    def blank(*shapes):
        return pl.pallas_call(
            lambda *refs: None,
            out_specs=[hbm] * len(shapes),
            out_shape=[like(*shape) for shape in shapes],
            name="blank",
        )()

    out_all, = blank((micros, rows, cols, dim))
    start = jnp.zeros((rows, wide, dim), BF16)
    out_piece = jnp.zeros((rows, half, dim), BF16)
    early, late = {}, {}
    steps = 2 * (sections - 1) + 1 + chunks
    pcol, act_two, s2, d3 = forward
    d_now, s2_now = d3[0], s2[0]
    sums, terms = [], None
    for step in range(steps):
        out_all, g3, g2, even, odd, g3_piece, g2_piece, s1_now = upper(
            step, early.get(step - 2, start), late.get(step - 3)
        )
        even_in, odd_in = exchange(even, odd)
        if terms is not None:
            sums = list(weights(step - 1, *terms, even, sums))
        if step % 2 and (step + 1) // 2 < micros:
            micro = (step + 1) // 2
            forward = second(micro, micro - 1, act_b, even_b, odd_b, forward, sums[2])
            pcol, act_two, s2, d3 = forward
        value, out_piece, g1_piece, d_now, s2_now = lower(
            step, g2, even_in, odd_in, g3, s1_now, sums[2] if sums else even
        )
        terms = (g3_piece, g2_piece, g1_piece)
        if step + 2 < steps:
            early[step] = lax.ppermute(value, ("section", "tile"), pairs_down)
        if sections - 2 <= step < sections - 2 + chunks:
            late[step] = lax.ppermute(early[step], "tile", pairs_z)
    sum_one, sum_two, sum_three = (v.astype(BF16) for v in weights(steps - 1, *terms, g1_piece, sums))
    out_all = flush(steps - 1)

    sizes = [dim * mid // tiles, 9 * mid * mid // tiles, mid * dim // tiles]
    x_size, z_size = 4, 2
    parts = jnp.concatenate(
        [v.reshape(tiles, n // 256, 256) for v, n in zip((sum_one, sum_two, sum_three), sizes)], axis=1
    ).reshape(x_size, z_size, 2, sum(sizes) // 256, 256)
    total = reduce_over_tiles(parts, x_size, z_size)
    cut = [0, sizes[0] // 256, (sizes[0] + sizes[1]) // 256, sum(sizes) // 256]
    one = total[cut[0] : cut[1]].reshape(1, dim // tiles, mid)
    two = total[cut[1] : cut[2]].reshape(1, 9 * mid // tiles, mid)
    three = total[cut[2] : cut[3]].reshape(1, mid // tiles, dim)
    return (out_all[None], one, two, three)


def solution(mesh):
    return jax.shard_map(
        local,
        mesh=mesh,
        in_specs=(
            P("section", None, "tile", None, None),
            P(None, "tile", None, None),
            P("section", None, None),
            P("section", None, None),
            P("section", None, None),
            P("section", None),
            P("section", None),
            P("section", None),
        ),
        out_specs=(
            P("section", None, "tile", None, None),
            P("section", "tile", None),
            P("section", "tile", None),
            P("section", "tile", None),
        ),
        check_vma=False,
    )
```

```python
import jax
import jax.numpy as jnp
from jax import lax
from jax.experimental import pallas as pl
from jax.experimental.pallas import tpu as pltpu
from jax.sharding import PartitionSpec as P

F32 = jnp.float32
BF16 = jnp.bfloat16
NT = (((1,), (1,)), ((), ()))
TN = (((0,), (0,)), ((), ()))
MIB = 1024 * 1024
BIG, SMALL = 24, 16


def silu_parts(v):
    s = 0.5 * jnp.tanh(0.5 * v) + 0.5
    return v * s, s * (1.0 + v * (1.0 - s))


def shifted(flat, width):
    n = flat.shape[0]
    col = lax.rem(lax.broadcasted_iota(jnp.int32, flat.shape, 0), width)
    left = jnp.where(col == 0, 0.0, pltpu.roll(flat, 1, 0))
    right = jnp.where(col == width - 1, 0.0, pltpu.roll(flat, n - 1, 0))
    return left, right


def spec(shape, index):
    return pl.BlockSpec(shape, index)


def fixed(shape):
    zeros = (0,) * len(shape)
    return pl.BlockSpec(shape, lambda *_: zeros)


def first_kernel(*refs, wide):
    base_ref, x_ref, w_ref, b_ref = refs[:4]
    act_ref, even_ref, odd_ref, s_ref = refs[-4:]
    _, rows, cols, dim = x_ref.shape
    pre = jnp.dot(x_ref[0].reshape(rows * cols, dim), w_ref[...], preferred_element_type=F32) + b_ref[...]
    act, slope = silu_parts(pre)
    act = act.reshape(rows, cols, -1)
    act_ref[0] = act.astype(BF16)
    odd = base_ref[4] == 1
    even_ref[0] = jnp.where(odd, act[0], act[rows - 1]).astype(BF16)
    odd_ref[0] = jnp.where(odd, act[rows - 1], act[0]).astype(BF16)
    slope = slope.reshape(rows, cols, -1)
    s_ref[0] = slope[:, :wide].astype(BF16)
    s_ref[1] = slope[:, cols - wide :].astype(BF16)


def second_kernel(*refs, wide):
    base_ref, act_ref, even_ref, odd_ref, x_ref, cot_ref, w2_ref, w3_ref, b2_ref, b3_ref = refs[:10]
    pcol_ref, act_two_ref, s_ref, d_ref = refs[-4:]
    _, rows, cols, dim = x_ref.shape
    mid = w3_ref.shape[0]
    pixels = rows * cols
    up, dn = edge_rows(base_ref, even_ref[0].astype(F32), odd_ref[0].astype(F32))
    rims = jnp.concatenate([up, act_ref[0].astype(F32).reshape(pixels, mid), dn], axis=0)
    left, right = shifted(rims, cols)
    pcol = jnp.concatenate([left.astype(BF16), rims.astype(BF16), right.astype(BF16)], axis=1)
    pcol_ref[0] = pcol.reshape(rows + 2, cols, 3 * mid)
    pre = b2_ref[...]
    for dy in range(3):
        pre = pre + jnp.dot(
            pcol[dy * cols : dy * cols + pixels],
            w2_ref[dy * 3 * mid : (dy + 1) * 3 * mid],
            preferred_element_type=F32,
        )
    act, slope = silu_parts(pre)
    slope = slope.reshape(rows, cols, mid)
    s_ref[0] = slope[:, :wide].astype(BF16)
    s_ref[1] = slope[:, cols - wide :].astype(BF16)
    act_two = act.astype(BF16)
    act_two_ref[0] = act.reshape(rows, cols, mid).astype(BF16)
    last = base_ref[1] == 1
    for r in range(rows):
        pre = jnp.dot(act_two[r * cols : (r + 1) * cols], w3_ref[...], preferred_element_type=F32)
        pre = pre + b3_ref[...] + x_ref[0, r].astype(F32)
        slope = silu_parts(pre)[1]
        slope = slope * jnp.where(last, cot_ref[0, r].astype(F32), 1.0)
        d_ref[0, r] = slope[:wide].astype(BF16)
        d_ref[1, r] = slope[cols - wide :].astype(BF16)


def start_if(cond, *copies):
    @pl.when(cond)
    def _():
        for copy in copies:
            copy.start()


def wait_if(cond, *copies):
    @pl.when(cond)
    def _():
        for copy in copies:
            copy.wait()


def place_of(step, base_ref, chunks):
    raw = step - base_ref[0]
    return jnp.clip(raw, 0, chunks - 1), jnp.logical_and(raw >= 0, raw < chunks)


def piece_of(array, chunk, half):
    where = pl.ds(pl.multiple_of(lax.rem(chunk, 2) * half, half), half)
    return array.at[lax.div(chunk, 2), :, where]


def upper_kernel(*refs, step, chunks, late):
    base_ref, early_ref, refs = refs[0], refs[1], refs[2:]
    if late:
        late_ref, refs = refs[0], refs[1:]
    d_ref, s2_ref, s1_ref, w3_ref, out_piece, _ = refs[:6]
    out_all, g3_ref, g2_ref, even_ref, odd_ref, g3_piece, g2_piece, s1_out, sems = refs[6:]
    rows, wide, dim = d_ref.shape
    half = g2_piece.shape[1]
    chunk, _ = place_of(step, base_ref, chunks)
    get_s = pltpu.make_async_copy(s1_ref.at[chunk], s1_out, sems.at[0])
    get_s.start()
    before, had = place_of(step - 1, base_ref, chunks)
    if step:
        put = pltpu.make_async_copy(out_piece, piece_of(out_all, before, half), sems.at[1])
        start_if(had, put)
    value = early_ref[...].astype(F32)
    if late:
        value = jnp.where(base_ref[5] == 1, late_ref[...].astype(F32), value)
    value = jnp.where(base_ref[1] == 1, 1.0, value)
    g3 = value * d_ref[...].astype(F32)
    g3_ref[...] = g3.astype(BF16)
    low = lax.rem(chunk, 2) == 0
    g3_piece[...] = jnp.where(low, g3[:, :half], g3[:, wide - half :]).astype(BF16)
    g3 = g3.reshape(rows * wide, dim).astype(BF16)
    g2 = lax.dot_general(g3, w3_ref[...], NT, preferred_element_type=F32)
    g2 = g2.reshape(rows, wide, -1) * s2_ref[...].astype(F32)
    g2_ref[...] = g2.astype(BF16)
    odd = base_ref[4] == 1
    even_ref[...] = jnp.where(odd, g2[0], g2[rows - 1]).astype(BF16)
    odd_ref[...] = jnp.where(odd, g2[rows - 1], g2[0]).astype(BF16)
    g2_piece[...] = jnp.where(low, g2[:, :half], g2[:, wide - half :]).astype(BF16)
    if step:
        wait_if(had, put)
    get_s.wait()


def lower_kernel(*refs, step, chunks, last):
    base_ref, g2_ref, even_ref, odd_ref, s1_ref, g3_ref, w2_ref, w1_ref, _ = refs[:9]
    if last:
        v_ref, out_piece, g1_piece = refs[9:]
    else:
        d_ref, s2_ref, v_ref, out_piece, g1_piece, d_out, s2_out, sems = refs[9:]
    rows, wide, mid = g2_ref.shape
    dim = w1_ref.shape[0]
    half = out_piece.shape[1]
    n = rows * wide
    chunk, _ = place_of(step, base_ref, chunks)
    gets = []
    if not last:
        later, _ = place_of(step + 1, base_ref, chunks)
        gets = [
            pltpu.make_async_copy(d_ref.at[later], d_out, sems.at[0]),
            pltpu.make_async_copy(s2_ref.at[later], s2_out, sems.at[1]),
        ]
    for get in gets:
        get.start()
    up, dn = edge_rows(base_ref, even_ref[...].astype(F32), odd_ref[...].astype(F32))
    rims = jnp.concatenate([up, g2_ref[...].astype(F32).reshape(n, mid), dn], axis=0)
    left, right = shifted(rims, wide)
    views = (right, rims, left)
    back = None
    for dy in range(3):
        start = (2 - dy) * wide
        for dx in range(3):
            tap = 3 * dy + dx
            part = lax.dot_general(
                views[dx][start : start + n].astype(BF16),
                w2_ref[tap * mid : (tap + 1) * mid],
                NT,
                preferred_element_type=F32,
            )
            back = part if back is None else back + part
    g1 = back * s1_ref[...].astype(F32).reshape(n, mid)
    g1_rows = g1.reshape(rows, wide, mid)
    low = lax.rem(chunk, 2) == 0
    g1_piece[...] = jnp.where(low, g1_rows[:, :half], g1_rows[:, wide - half :]).astype(BF16)
    total = lax.dot_general(g1.astype(BF16), w1_ref[...], NT, preferred_element_type=F32)
    total = total.reshape(rows, wide, dim) + g3_ref[...].astype(F32)
    v_ref[...] = total.astype(BF16)
    out_piece[...] = jnp.where(low, total[:, :half], total[:, wide - half :]).astype(BF16)
    for get in gets:
        get.wait()


def flush_kernel(base_ref, out_piece, out_in, out_all, sem, *, step, chunks):
    chunk, live = place_of(step, base_ref, chunks)
    put = pltpu.make_async_copy(out_piece, piece_of(out_all, chunk, out_piece.shape[1]), sem)
    start_if(live, put)
    wait_if(live, put)


def weights_kernel(*refs, step, chunks):
    base_ref, x_ref, pcol_ref, act_ref, g3_ref, g2_ref, g1_ref, _ = refs[:8]
    olds, (one, two, three, x_buf, p_buf, a_buf, sems) = refs[8:-7], refs[-7:]
    rows, half, dim = x_buf.shape
    mid = a_buf.shape[2]
    chunk, live = place_of(step, base_ref, chunks)
    gets = [
        pltpu.make_async_copy(piece_of(src, chunk, half), dst, sems.at[i])
        for i, (src, dst) in enumerate(((x_ref, x_buf), (pcol_ref, p_buf), (act_ref, a_buf)))
    ]
    start_if(live, *gets)
    pixels = rows * half

    def put(ref, old, place, term):
        ref[place] = term if old is None else old[place] + term

    old_one, old_two, old_three = olds if olds else (None, None, None)

    @pl.when(live)
    def _():
        for get in gets:
            get.wait()
        g3 = g3_ref[...].reshape(pixels, dim)
        g2 = g2_ref[...].reshape(pixels, mid)
        g1 = g1_ref[...].reshape(pixels, mid)
        all_rows = slice(None)
        put(three, old_three, all_rows, lax.dot_general(
            a_buf[...].reshape(pixels, mid), g3, TN, preferred_element_type=F32))
        put(one, old_one, all_rows, lax.dot_general(
            x_buf[...].reshape(pixels, dim), g1, TN, preferred_element_type=F32))
        for dy in range(3):
            put(two, old_two, slice(dy * 3 * mid, (dy + 1) * 3 * mid), lax.dot_general(
                p_buf[dy : dy + rows].reshape(pixels, 3 * mid), g2, TN, preferred_element_type=F32))

    @pl.when(jnp.logical_not(live))
    def _():
        for ref, old in ((one, old_one), (two, old_two), (three, old_three)):
            ref[...] = jnp.zeros_like(ref) if old is None else old[...]


def edge_rows(base_ref, even, odd):
    flip = base_ref[4] == 1
    up = jnp.where(base_ref[2] == 1, jnp.where(flip, even, odd), 0.0)
    dn = jnp.where(base_ref[3] == 1, jnp.where(flip, odd, even), 0.0)
    return up, dn


def pack_kernel(base_ref, one_ref, two_ref, three_ref, send_ref, keep_ref):
    blocks, lines, width = send_ref.shape
    odd = base_ref[4] == 1
    tiles = 2 * blocks

    def block(ref, i):
        size = ref.shape[0] // tiles
        a, b = (ref[(2 * i + j) * size : (2 * i + j + 1) * size] for j in range(2))
        return jnp.where(odd, a, b).astype(BF16), jnp.where(odd, b, a).astype(BF16)

    for i in range(blocks):
        at = 0
        for ref in (one_ref, two_ref, three_ref):
            pair = block(ref, i)
            size = pair[0].shape[0]
            for j in range(ref.shape[1] // width):
                for out, value in zip((send_ref, keep_ref), pair):
                    out[i, at : at + size] = value[:, j * width : (j + 1) * width]
                at += size


def finish_kernel(*refs):
    terms, (one_ref, two_ref, three_ref) = refs[:-3], refs[-3:]
    total = terms[0][...].astype(F32)
    for term in terms[1:]:
        total = total + term[...].astype(F32)
    width = total.shape[1]
    at = 0
    for ref in (one_ref, two_ref, three_ref):
        size = ref.shape[0]
        for j in range(ref.shape[1] // width):
            ref[:, j * width : (j + 1) * width] = total[at : at + size]
            at += size


def chip_terms(both, x_size, z_size):
    me = lax.axis_index("tile")
    z, x = (me // 2) % z_size, me // (2 * z_size)
    count = 2 * x_size * z_size

    def at(dx, dz):
        return lax.dynamic_index_in_dim(both, (x + dx) % x_size * z_size + (z + dz) % z_size, 0, keepdims=False)

    def target(i, dx, dz):
        ic, iz, ix = i % 2, (i // 2) % z_size, i // (2 * z_size)
        return (((ix + dx) % x_size) * z_size + (iz + dz) % z_size) * 2 + ic

    terms = [at(0, 0)]
    for dz in range(z_size - 1, -1, -1):
        for dx in sorted(range(x_size), key=lambda d: -min(d, x_size - d)):
            if dx or dz:
                terms.append(lax.ppermute(at(dx, dz), "tile", [(i, target(i, dx, dz)) for i in range(count)]))
    return terms


def local(
    stored_inputs, cotangent, w_reduce, w_spatial, w_expand, bias_reduce, bias_spatial, bias_expand
):
    x_all = stored_inputs[0]
    micros, rows, cols, dim = x_all.shape
    w1, w2, w3 = w_reduce[0], w_spatial[0], w_expand[0]
    mid = w1.shape[1]
    sections, tiles = lax.axis_size("section"), lax.axis_size("tile")
    me, tile = lax.axis_index("section"), lax.axis_index("tile")
    half = cols // 2
    wide = half + sections
    chunks = 2 * micros
    cross = sections // 2
    base = jnp.stack([
        2 * (sections - 1 - me) + (me < cross),
        me == sections - 1,
        tile > 0,
        tile < tiles - 1,
        tile % 2,
        me == cross - 1,
    ]).astype(jnp.int32)
    pairs_even = [(t, t ^ 1) for t in range(tiles)]
    ends = (0, tiles - 1)
    pairs_odd = [(t, t if t in ends else t + 1 if t % 2 else t - 1) for t in range(tiles)]
    pairs_z = [(t, t ^ 2) for t in range(tiles)]
    pairs_down = [
        (s * tiles + t, (s - 1) % sections * tiles + (t if s % cross else t ^ 2))
        for s in range(sections)
        for t in range(tiles)
    ]

    def exchange(even, odd):
        return lax.ppermute(even, "tile", pairs_even), lax.ppermute(odd, "tile", pairs_odd)

    big = pltpu.CompilerParams(vmem_limit_bytes=BIG * MIB)
    small = pltpu.CompilerParams(vmem_limit_bytes=SMALL * MIB)
    smem = pl.BlockSpec(memory_space=pltpu.SMEM)
    vmem = pl.BlockSpec(memory_space=pltpu.VMEM)
    hbm = pl.BlockSpec(memory_space=pltpu.HBM)
    anywhere = pl.BlockSpec(memory_space=pl.ANY)

    def like(*shape):
        return jax.ShapeDtypeStruct(shape, BF16)

    def first(begin, end, s_in, after):
        extra = [] if s_in is None else [s_in, after]
        count = end - begin
        return pl.pallas_call(
            lambda *refs: first_kernel(*refs, wide=wide),
            grid=(count,),
            in_specs=[
                smem,
                spec((1, rows, cols, dim), lambda m: (m + begin, 0, 0, 0)),
                fixed((dim, mid)),
                fixed((1, mid)),
            ] + ([hbm, anywhere] if extra else []),
            out_specs=[
                spec((1, rows, cols, mid), lambda m: (m, 0, 0, 0)),
                spec((1, cols, mid), lambda m: (m, 0, 0)),
                spec((1, cols, mid), lambda m: (m, 0, 0)),
                spec((2, rows, wide, mid), lambda m: (m + begin, 0, 0, 0)),
            ],
            out_shape=[
                like(count, rows, cols, mid),
                like(count, cols, mid),
                like(count, cols, mid),
                like(chunks, rows, wide, mid),
            ],
            input_output_aliases={4: 3} if extra else {},
            compiler_params=big,
            name="first",
        )(base, x_all, w1, bias_reduce, *extra)

    def second(micro, at, act, even, odd, earlier, after):
        extra = [] if earlier is None else [*earlier, after]
        return pl.pallas_call(
            lambda *refs: second_kernel(*refs, wide=wide),
            grid=(1,),
            in_specs=[
                smem,
                spec((1, rows, cols, mid), lambda m: (at, 0, 0, 0)),
                spec((1, cols, mid), lambda m: (at, 0, 0)),
                spec((1, cols, mid), lambda m: (at, 0, 0)),
                spec((1, rows, cols, dim), lambda m: (micro, 0, 0, 0)),
                spec((1, rows, cols, dim), lambda m: (micro, 0, 0, 0)),
                fixed((9 * mid, mid)),
                fixed((mid, dim)),
                fixed((1, mid)),
                fixed((1, dim)),
            ] + ([hbm] * 4 + [anywhere] if extra else []),
            out_specs=[
                spec((1, rows + 2, cols, 3 * mid), lambda m: (micro, 0, 0, 0)),
                spec((1, rows, cols, mid), lambda m: (micro, 0, 0, 0)),
                spec((2, rows, wide, mid), lambda m: (micro, 0, 0, 0)),
                spec((2, rows, wide, dim), lambda m: (micro, 0, 0, 0)),
            ],
            out_shape=[
                like(micros, rows + 2, cols, 3 * mid),
                like(micros, rows, cols, mid),
                like(chunks, rows, wide, mid),
                like(chunks, rows, wide, dim),
            ],
            input_output_aliases={10: 0, 11: 1, 12: 2, 13: 3} if extra else {},
            compiler_params=big,
            name="second",
        )(base, act, even, odd, x_all, cotangent, w2, w3, bias_spatial, bias_expand, *extra)

    def upper(step, early, late):
        values = [early] if late is None else [early, late]
        k = len(values)
        return pl.pallas_call(
            lambda *refs: upper_kernel(*refs, step=step, chunks=chunks, late=late is not None),
            in_specs=[smem] + [vmem] * k + [vmem, vmem, hbm, vmem, vmem, hbm],
            out_specs=[hbm] + [vmem] * 7,
            out_shape=[
                like(*out_all.shape),
                like(rows, wide, dim),
                like(rows, wide, mid),
                like(wide, mid),
                like(wide, mid),
                like(rows, half, dim),
                like(rows, half, mid),
                like(rows, wide, mid),
            ],
            scratch_shapes=[pltpu.SemaphoreType.DMA((2,))],
            input_output_aliases={6 + k: 0},
            compiler_params=small,
            name="upper",
        )(base, *values, d_now, s2_now, s1, w3, out_piece, out_all)

    steps = 2 * (sections - 1) + 1 + chunks

    def lower(step, g2, even, odd, g3, s1_now, after):
        last = step == steps - 1
        outs = [
            like(rows, wide, dim),
            like(rows, half, dim),
            like(rows, half, mid),
            like(rows, wide, dim),
            like(rows, wide, mid),
        ]
        outs = outs[:3] if last else outs
        got = pl.pallas_call(
            lambda *refs: lower_kernel(*refs, step=step, chunks=chunks, last=last),
            in_specs=[smem] + [vmem] * 7 + [anywhere] + ([] if last else [hbm] * 2),
            out_specs=[vmem] * len(outs),
            out_shape=outs,
            scratch_shapes=[] if last else [pltpu.SemaphoreType.DMA((2,))],
            compiler_params=small,
            name="lower",
        )(base, g2, even, odd, s1_now, g3, w2, w1, after, *([] if last else [d3, s2]))
        return (*got, None, None) if last else got

    def flush(step):
        return pl.pallas_call(
            lambda *refs: flush_kernel(*refs, step=step, chunks=chunks),
            in_specs=[smem, vmem, hbm],
            out_specs=hbm,
            out_shape=like(*out_all.shape),
            scratch_shapes=[pltpu.SemaphoreType.DMA],
            input_output_aliases={2: 0},
            compiler_params=small,
            name="flush",
        )(base, out_piece, out_all)

    def weights(step, g3, g2, g1, after, olds):
        shapes = [(dim, mid), (9 * mid, mid), (mid, dim)]
        return pl.pallas_call(
            lambda *refs: weights_kernel(*refs, step=step, chunks=chunks),
            in_specs=[smem, hbm, hbm, hbm, vmem, vmem, vmem, anywhere] + [vmem] * len(olds),
            out_specs=[vmem] * 3,
            out_shape=[jax.ShapeDtypeStruct(shape, F32) for shape in shapes],
            scratch_shapes=[
                pltpu.VMEM((rows, half, dim), BF16),
                pltpu.VMEM((rows + 2, half, 3 * mid), BF16),
                pltpu.VMEM((rows, half, mid), BF16),
                pltpu.SemaphoreType.DMA((3,)),
            ],
            input_output_aliases={8: 0, 9: 1, 10: 2} if olds else {},
            compiler_params=small,
            name="weights",
        )(base, x_all, pcol, act_two, g3, g2, g1, after, *olds)

    act_a, even, odd, s1 = first(0, 1, None, None)
    even_a, odd_a = exchange(even, odd)
    forward = second(0, 0, act_a, even_a, odd_a, None, None)

    def blank(*shapes):
        return pl.pallas_call(
            lambda *refs: None,
            out_specs=[hbm] * len(shapes),
            out_shape=[like(*shape) for shape in shapes],
            name="blank",
        )()

    out_all, = blank((micros, rows, cols, dim))
    start = jnp.zeros((rows, wide, dim), BF16)
    out_piece = jnp.zeros((rows, half, dim), BF16)
    early, late = {}, {}
    pcol, act_two, s2, d3 = forward
    d_now, s2_now = d3[0], s2[0]
    sums, terms = [], None
    for step in range(steps):
        out_all, g3, g2, even, odd, g3_piece, g2_piece, s1_now = upper(
            step, early.get(step - 2, start), late.get(step - 3)
        )
        even_in, odd_in = exchange(even, odd)
        if terms is not None:
            sums = list(weights(step - 1, *terms, even, sums))
        if step % 2 and (step + 1) // 2 < micros:
            micro = (step + 1) // 2
            forward = second(micro, micro - 1, act_b, even_b, odd_b, forward, sums[2])
            pcol, act_two, s2, d3 = forward
        value, out_piece, g1_piece, d_now, s2_now = lower(
            step, g2, even_in, odd_in, g3, s1_now, sums[2] if sums else even
        )
        terms = (g3_piece, g2_piece, g1_piece)
        if step == 0:
            act_b, even, odd, s1 = first(1, micros, s1, g1_piece)
            even_b, odd_b = exchange(even, odd)
        if step + 2 < steps:
            early[step] = lax.ppermute(value, ("section", "tile"), pairs_down)
        if sections - 2 <= step < sections - 2 + chunks:
            late[step] = lax.ppermute(early[step], "tile", pairs_z)
    sums = weights(steps - 1, *terms, g1_piece, sums)
    lines = (dim + 9 * mid + dim) // tiles
    send, keep = pl.pallas_call(
        pack_kernel,
        in_specs=[smem, vmem, vmem, vmem],
        out_specs=[vmem, vmem],
        out_shape=[like(tiles // 2, lines, mid)] * 2,
        compiler_params=small,
        name="pack",
    )(base, *sums)
    came = lax.ppermute(send, "tile", pairs_even)
    both = (keep.astype(F32) + came.astype(F32)).astype(BF16)
    x_size, z_size = 4, 2
    shares = chip_terms(both, x_size, z_size)
    out_all = flush(steps - 1)
    one, two, three = pl.pallas_call(
        finish_kernel,
        in_specs=[vmem] * len(shares),
        out_specs=[vmem] * 3,
        out_shape=[
            jax.ShapeDtypeStruct((dim // tiles, mid), F32),
            jax.ShapeDtypeStruct((9 * mid // tiles, mid), F32),
            jax.ShapeDtypeStruct((mid // tiles, dim), F32),
        ],
        compiler_params=small,
        name="finish",
    )(*shares)
    return (out_all[None], one[None], two[None], three[None])


def solution(mesh):
    return jax.shard_map(
        local,
        mesh=mesh,
        in_specs=(
            P("section", None, "tile", None, None),
            P(None, "tile", None, None),
            P("section", None, None),
            P("section", None, None),
            P("section", None, None),
            P("section", None),
            P("section", None),
            P("section", None),
        ),
        out_specs=(
            P("section", None, "tile", None, None),
            P("section", "tile", None),
            P("section", "tile", None),
            P("section", "tile", None),
        ),
        check_vma=False,
    )
```

```python
import jax
import jax.numpy as jnp
from jax import lax
from jax.experimental import pallas as pl
from jax.experimental.pallas import tpu as pltpu
from jax.sharding import PartitionSpec as P

F32 = jnp.float32
BF16 = jnp.bfloat16
NT = (((1,), (1,)), ((), ()))
TN = (((0,), (0,)), ((), ()))
MIB = 1024 * 1024
BIG, SMALL = 24, 16


def silu_parts(v):
    s = 0.5 * jnp.tanh(0.5 * v) + 0.5
    return v * s, s * (1.0 + v * (1.0 - s))


def shifted(flat, width):
    n = flat.shape[0]
    col = lax.rem(lax.broadcasted_iota(jnp.int32, flat.shape, 0), width)
    left = jnp.where(col == 0, 0.0, pltpu.roll(flat, 1, 0))
    right = jnp.where(col == width - 1, 0.0, pltpu.roll(flat, n - 1, 0))
    return left, right


def spec(shape, index):
    return pl.BlockSpec(shape, index)


def fixed(shape):
    zeros = (0,) * len(shape)
    return pl.BlockSpec(shape, lambda *_: zeros)


def first_kernel(*refs, wide):
    base_ref, x_ref, w_ref, b_ref = refs[:4]
    act_ref, even_ref, odd_ref, s_ref = refs[-4:]
    _, rows, cols, dim = x_ref.shape
    pre = jnp.dot(x_ref[0].reshape(rows * cols, dim), w_ref[...], preferred_element_type=F32) + b_ref[...]
    act, slope = silu_parts(pre)
    act = act.reshape(rows, cols, -1)
    act_ref[0] = act.astype(BF16)
    odd = base_ref[4] == 1
    even_ref[0] = jnp.where(odd, act[0], act[rows - 1]).astype(BF16)
    odd_ref[0] = jnp.where(odd, act[rows - 1], act[0]).astype(BF16)
    slope = slope.reshape(rows, cols, -1)
    s_ref[0] = slope[:, :wide].astype(BF16)
    s_ref[1] = slope[:, cols - wide :].astype(BF16)


def second_kernel(*refs, wide):
    base_ref, act_ref, even_ref, odd_ref, x_ref, cot_ref, w2_ref, w3_ref, b2_ref, b3_ref = refs[:10]
    pcol_ref, act_two_ref, s_ref, d_ref = refs[-4:]
    _, rows, cols, dim = x_ref.shape
    mid = w3_ref.shape[0]
    pixels = rows * cols
    up, dn = edge_rows(base_ref, even_ref[0].astype(F32), odd_ref[0].astype(F32))
    rims = jnp.concatenate([up, act_ref[0].astype(F32).reshape(pixels, mid), dn], axis=0)
    left, right = shifted(rims, cols)
    pcol = jnp.concatenate([left.astype(BF16), rims.astype(BF16), right.astype(BF16)], axis=1)
    pcol_ref[0] = pcol.reshape(rows + 2, cols, 3 * mid)
    pre = b2_ref[...]
    for dy in range(3):
        pre = pre + jnp.dot(
            pcol[dy * cols : dy * cols + pixels],
            w2_ref[dy * 3 * mid : (dy + 1) * 3 * mid],
            preferred_element_type=F32,
        )
    act, slope = silu_parts(pre)
    slope = slope.reshape(rows, cols, mid)
    s_ref[0] = slope[:, :wide].astype(BF16)
    s_ref[1] = slope[:, cols - wide :].astype(BF16)
    act_two = act.astype(BF16)
    act_two_ref[0] = act.reshape(rows, cols, mid).astype(BF16)
    last = base_ref[1] == 1
    for r in range(rows):
        pre = jnp.dot(act_two[r * cols : (r + 1) * cols], w3_ref[...], preferred_element_type=F32)
        pre = pre + b3_ref[...] + x_ref[0, r].astype(F32)
        slope = silu_parts(pre)[1]
        slope = slope * jnp.where(last, cot_ref[0, r].astype(F32), 1.0)
        d_ref[0, r] = slope[:wide].astype(BF16)
        d_ref[1, r] = slope[cols - wide :].astype(BF16)


def start_if(cond, *copies):
    @pl.when(cond)
    def _():
        for copy in copies:
            copy.start()


def wait_if(cond, *copies):
    @pl.when(cond)
    def _():
        for copy in copies:
            copy.wait()


def place_of(step, base_ref, chunks):
    raw = step - base_ref[0]
    return jnp.clip(raw, 0, chunks - 1), jnp.logical_and(raw >= 0, raw < chunks)


def piece_of(array, chunk, half):
    where = pl.ds(pl.multiple_of(lax.rem(chunk, 2) * half, half), half)
    return array.at[lax.div(chunk, 2), :, where]


def upper_kernel(*refs, step, chunks, late):
    base_ref, early_ref, refs = refs[0], refs[1], refs[2:]
    if late:
        late_ref, refs = refs[0], refs[1:]
    d_ref, s2_ref, s1_ref, w3_ref, out_piece, _ = refs[:6]
    out_all, g3_ref, g2_ref, even_ref, odd_ref, g3_piece, g2_piece, s1_out, sems = refs[6:]
    rows, wide, dim = d_ref.shape
    half = g2_piece.shape[1]
    chunk, _ = place_of(step, base_ref, chunks)
    get_s = pltpu.make_async_copy(s1_ref.at[chunk], s1_out, sems.at[0])
    get_s.start()
    before, had = place_of(step - 1, base_ref, chunks)
    if step:
        put = pltpu.make_async_copy(out_piece, piece_of(out_all, before, half), sems.at[1])
        start_if(had, put)
    value = early_ref[...].astype(F32)
    if late:
        value = jnp.where(base_ref[5] == 1, late_ref[...].astype(F32), value)
    value = jnp.where(base_ref[1] == 1, 1.0, value)
    g3 = value * d_ref[...].astype(F32)
    g3_ref[...] = g3.astype(BF16)
    low = lax.rem(chunk, 2) == 0
    g3_piece[...] = jnp.where(low, g3[:, :half], g3[:, wide - half :]).astype(BF16)
    g3 = g3.reshape(rows * wide, dim).astype(BF16)
    g2 = lax.dot_general(g3, w3_ref[...], NT, preferred_element_type=F32)
    g2 = g2.reshape(rows, wide, -1) * s2_ref[...].astype(F32)
    g2_ref[...] = g2.astype(BF16)
    odd = base_ref[4] == 1
    even_ref[...] = jnp.where(odd, g2[0], g2[rows - 1]).astype(BF16)
    odd_ref[...] = jnp.where(odd, g2[rows - 1], g2[0]).astype(BF16)
    g2_piece[...] = jnp.where(low, g2[:, :half], g2[:, wide - half :]).astype(BF16)
    if step:
        wait_if(had, put)
    get_s.wait()


def lower_kernel(*refs, step, chunks, last):
    base_ref, g2_ref, even_ref, odd_ref, s1_ref, g3_ref, w2_ref, w1_ref, _ = refs[:9]
    if last:
        v_ref, out_piece, g1_piece = refs[9:]
    else:
        d_ref, s2_ref, v_ref, out_piece, g1_piece, d_out, s2_out, sems = refs[9:]
    rows, wide, mid = g2_ref.shape
    dim = w1_ref.shape[0]
    half = out_piece.shape[1]
    n = rows * wide
    chunk, _ = place_of(step, base_ref, chunks)
    gets = []
    if not last:
        later, _ = place_of(step + 1, base_ref, chunks)
        gets = [
            pltpu.make_async_copy(d_ref.at[later], d_out, sems.at[0]),
            pltpu.make_async_copy(s2_ref.at[later], s2_out, sems.at[1]),
        ]
    for get in gets:
        get.start()
    up, dn = edge_rows(base_ref, even_ref[...].astype(F32), odd_ref[...].astype(F32))
    rims = jnp.concatenate([up, g2_ref[...].astype(F32).reshape(n, mid), dn], axis=0)
    left, right = shifted(rims, wide)
    views = (right, rims, left)
    back = None
    for dy in range(3):
        start = (2 - dy) * wide
        for dx in range(3):
            tap = 3 * dy + dx
            part = lax.dot_general(
                views[dx][start : start + n].astype(BF16),
                w2_ref[tap * mid : (tap + 1) * mid],
                NT,
                preferred_element_type=F32,
            )
            back = part if back is None else back + part
    g1 = back * s1_ref[...].astype(F32).reshape(n, mid)
    g1_rows = g1.reshape(rows, wide, mid)
    low = lax.rem(chunk, 2) == 0
    g1_piece[...] = jnp.where(low, g1_rows[:, :half], g1_rows[:, wide - half :]).astype(BF16)
    total = lax.dot_general(g1.astype(BF16), w1_ref[...], NT, preferred_element_type=F32)
    total = total.reshape(rows, wide, dim) + g3_ref[...].astype(F32)
    v_ref[...] = total.astype(BF16)
    out_piece[...] = jnp.where(low, total[:, :half], total[:, wide - half :]).astype(BF16)
    for get in gets:
        get.wait()


def flush_kernel(base_ref, out_piece, out_in, out_all, sem, *, step, chunks):
    chunk, live = place_of(step, base_ref, chunks)
    put = pltpu.make_async_copy(out_piece, piece_of(out_all, chunk, out_piece.shape[1]), sem)
    start_if(live, put)
    wait_if(live, put)


def weights_kernel(*refs, step, chunks):
    base_ref, x_ref, pcol_ref, act_ref, g3_ref, g2_ref, g1_ref, _ = refs[:8]
    olds, (one, two, three, x_buf, p_buf, a_buf, sems) = refs[8:-7], refs[-7:]
    rows, half, dim = x_buf.shape
    mid = a_buf.shape[2]
    chunk, live = place_of(step, base_ref, chunks)
    gets = [
        pltpu.make_async_copy(piece_of(src, chunk, half), dst, sems.at[i])
        for i, (src, dst) in enumerate(((x_ref, x_buf), (pcol_ref, p_buf), (act_ref, a_buf)))
    ]
    start_if(live, *gets)
    pixels = rows * half

    def put(ref, old, place, term):
        ref[place] = term if old is None else old[place] + term

    old_one, old_two, old_three = olds if olds else (None, None, None)

    @pl.when(live)
    def _():
        for get in gets:
            get.wait()
        g3 = g3_ref[...].reshape(pixels, dim)
        g2 = g2_ref[...].reshape(pixels, mid)
        g1 = g1_ref[...].reshape(pixels, mid)
        all_rows = slice(None)
        put(three, old_three, all_rows, lax.dot_general(
            a_buf[...].reshape(pixels, mid), g3, TN, preferred_element_type=F32))
        put(one, old_one, all_rows, lax.dot_general(
            x_buf[...].reshape(pixels, dim), g1, TN, preferred_element_type=F32))
        for dy in range(3):
            put(two, old_two, slice(dy * 3 * mid, (dy + 1) * 3 * mid), lax.dot_general(
                p_buf[dy : dy + rows].reshape(pixels, 3 * mid), g2, TN, preferred_element_type=F32))

    @pl.when(jnp.logical_not(live))
    def _():
        for ref, old in ((one, old_one), (two, old_two), (three, old_three)):
            ref[...] = jnp.zeros_like(ref) if old is None else old[...]


def edge_rows(base_ref, even, odd):
    flip = base_ref[4] == 1
    up = jnp.where(base_ref[2] == 1, jnp.where(flip, even, odd), 0.0)
    dn = jnp.where(base_ref[3] == 1, jnp.where(flip, odd, even), 0.0)
    return up, dn


def pack_kernel(base_ref, one_ref, two_ref, three_ref, send_ref, keep_ref):
    blocks, lines, width = send_ref.shape
    odd = base_ref[4] == 1
    tiles = 2 * blocks

    def block(ref, i):
        size = ref.shape[0] // tiles
        a, b = (ref[(2 * i + j) * size : (2 * i + j + 1) * size] for j in range(2))
        return jnp.where(odd, a, b).astype(BF16), jnp.where(odd, b, a).astype(BF16)

    for i in range(blocks):
        at = 0
        for ref in (one_ref, two_ref, three_ref):
            pair = block(ref, i)
            size = pair[0].shape[0]
            for j in range(ref.shape[1] // width):
                for out, value in zip((send_ref, keep_ref), pair):
                    out[i, at : at + size] = value[:, j * width : (j + 1) * width]
                at += size


def finish_kernel(*refs):
    terms, (one_ref, two_ref, three_ref) = refs[:-3], refs[-3:]
    total = terms[0][...].astype(F32)
    for term in terms[1:]:
        total = total + term[...].astype(F32)
    width = total.shape[1]
    at = 0
    for ref in (one_ref, two_ref, three_ref):
        size = ref.shape[0]
        for j in range(ref.shape[1] // width):
            ref[:, j * width : (j + 1) * width] = total[at : at + size]
            at += size


def chip_terms(both, x_size, z_size):
    me = lax.axis_index("tile")
    z, x = (me // 2) % z_size, me // (2 * z_size)
    count = 2 * x_size * z_size

    def at(dx, dz):
        return lax.dynamic_index_in_dim(both, (x + dx) % x_size * z_size + (z + dz) % z_size, 0, keepdims=False)

    def target(i, dx, dz):
        ic, iz, ix = i % 2, (i // 2) % z_size, i // (2 * z_size)
        return (((ix + dx) % x_size) * z_size + (iz + dz) % z_size) * 2 + ic

    terms = [at(0, 0)]
    for dz in range(z_size - 1, -1, -1):
        for dx in sorted(range(x_size), key=lambda d: -min(d, x_size - d)):
            if dx or dz:
                terms.append(lax.ppermute(at(dx, dz), "tile", [(i, target(i, dx, dz)) for i in range(count)]))
    return terms


def local(
    stored_inputs, cotangent, w_reduce, w_spatial, w_expand, bias_reduce, bias_spatial, bias_expand
):
    x_all = stored_inputs[0]
    micros, rows, cols, dim = x_all.shape
    w1, w2, w3 = w_reduce[0], w_spatial[0], w_expand[0]
    mid = w1.shape[1]
    sections, tiles = lax.axis_size("section"), lax.axis_size("tile")
    me, tile = lax.axis_index("section"), lax.axis_index("tile")
    half = cols // 2
    wide = half + sections
    chunks = 2 * micros
    cross = sections // 2
    base = jnp.stack([
        2 * (sections - 1 - me) + (me < cross),
        me == sections - 1,
        tile > 0,
        tile < tiles - 1,
        tile % 2,
        me == cross - 1,
    ]).astype(jnp.int32)
    pairs_even = [(t, t ^ 1) for t in range(tiles)]
    ends = (0, tiles - 1)
    pairs_odd = [(t, t if t in ends else t + 1 if t % 2 else t - 1) for t in range(tiles)]
    pairs_z = [((cross - 1) * tiles + t, (cross - 1) * tiles + (t ^ 2)) for t in range(tiles)]
    pairs_down = [
        (s * tiles + t, (s - 1) % sections * tiles + (t if s % cross else t ^ 2))
        for s in range(sections)
        for t in range(tiles)
    ]

    def exchange(even, odd):
        return lax.ppermute(even, "tile", pairs_even), lax.ppermute(odd, "tile", pairs_odd)

    big = pltpu.CompilerParams(vmem_limit_bytes=BIG * MIB)
    small = pltpu.CompilerParams(vmem_limit_bytes=SMALL * MIB)
    smem = pl.BlockSpec(memory_space=pltpu.SMEM)
    vmem = pl.BlockSpec(memory_space=pltpu.VMEM)
    hbm = pl.BlockSpec(memory_space=pltpu.HBM)
    anywhere = pl.BlockSpec(memory_space=pl.ANY)

    def like(*shape):
        return jax.ShapeDtypeStruct(shape, BF16)

    def first(begin, end, s_in, after):
        extra = [] if s_in is None else [s_in, after]
        count = end - begin
        return pl.pallas_call(
            lambda *refs: first_kernel(*refs, wide=wide),
            grid=(count,),
            in_specs=[
                smem,
                spec((1, rows, cols, dim), lambda m: (m + begin, 0, 0, 0)),
                fixed((dim, mid)),
                fixed((1, mid)),
            ] + ([hbm, anywhere] if extra else []),
            out_specs=[
                spec((1, rows, cols, mid), lambda m: (m, 0, 0, 0)),
                spec((1, cols, mid), lambda m: (m, 0, 0)),
                spec((1, cols, mid), lambda m: (m, 0, 0)),
                spec((2, rows, wide, mid), lambda m: (m + begin, 0, 0, 0)),
            ],
            out_shape=[
                like(count, rows, cols, mid),
                like(count, cols, mid),
                like(count, cols, mid),
                like(chunks, rows, wide, mid),
            ],
            input_output_aliases={4: 3} if extra else {},
            compiler_params=big,
            name="first",
        )(base, x_all, w1, bias_reduce, *extra)

    def second(micro, at, act, even, odd, earlier, after):
        extra = [] if earlier is None else [*earlier, after]
        return pl.pallas_call(
            lambda *refs: second_kernel(*refs, wide=wide),
            grid=(1,),
            in_specs=[
                smem,
                spec((1, rows, cols, mid), lambda m: (at, 0, 0, 0)),
                spec((1, cols, mid), lambda m: (at, 0, 0)),
                spec((1, cols, mid), lambda m: (at, 0, 0)),
                spec((1, rows, cols, dim), lambda m: (micro, 0, 0, 0)),
                spec((1, rows, cols, dim), lambda m: (micro, 0, 0, 0)),
                fixed((9 * mid, mid)),
                fixed((mid, dim)),
                fixed((1, mid)),
                fixed((1, dim)),
            ] + ([hbm] * 4 + [anywhere] if extra else []),
            out_specs=[
                spec((1, rows + 2, cols, 3 * mid), lambda m: (micro, 0, 0, 0)),
                spec((1, rows, cols, mid), lambda m: (micro, 0, 0, 0)),
                spec((2, rows, wide, mid), lambda m: (micro, 0, 0, 0)),
                spec((2, rows, wide, dim), lambda m: (micro, 0, 0, 0)),
            ],
            out_shape=[
                like(micros, rows + 2, cols, 3 * mid),
                like(micros, rows, cols, mid),
                like(chunks, rows, wide, mid),
                like(chunks, rows, wide, dim),
            ],
            input_output_aliases={10: 0, 11: 1, 12: 2, 13: 3} if extra else {},
            compiler_params=big,
            name="second",
        )(base, act, even, odd, x_all, cotangent, w2, w3, bias_spatial, bias_expand, *extra)

    def upper(step, early, late):
        values = [early] if late is None else [early, late]
        k = len(values)
        return pl.pallas_call(
            lambda *refs: upper_kernel(*refs, step=step, chunks=chunks, late=late is not None),
            in_specs=[smem] + [vmem] * k + [vmem, vmem, hbm, vmem, vmem, hbm],
            out_specs=[hbm] + [vmem] * 7,
            out_shape=[
                like(*out_all.shape),
                like(rows, wide, dim),
                like(rows, wide, mid),
                like(wide, mid),
                like(wide, mid),
                like(rows, half, dim),
                like(rows, half, mid),
                like(rows, wide, mid),
            ],
            scratch_shapes=[pltpu.SemaphoreType.DMA((2,))],
            input_output_aliases={6 + k: 0},
            compiler_params=small,
            name="upper",
        )(base, *values, d_now, s2_now, s1, w3, out_piece, out_all)

    steps = 2 * (sections - 1) + 1 + chunks

    def lower(step, g2, even, odd, g3, s1_now, after):
        last = step == steps - 1
        outs = [
            like(rows, wide, dim),
            like(rows, half, dim),
            like(rows, half, mid),
            like(rows, wide, dim),
            like(rows, wide, mid),
        ]
        outs = outs[:3] if last else outs
        got = pl.pallas_call(
            lambda *refs: lower_kernel(*refs, step=step, chunks=chunks, last=last),
            in_specs=[smem] + [vmem] * 7 + [anywhere] + ([] if last else [hbm] * 2),
            out_specs=[vmem] * len(outs),
            out_shape=outs,
            scratch_shapes=[] if last else [pltpu.SemaphoreType.DMA((2,))],
            compiler_params=small,
            name="lower",
        )(base, g2, even, odd, s1_now, g3, w2, w1, after, *([] if last else [d3, s2]))
        return (*got, None, None) if last else got

    def flush(step):
        return pl.pallas_call(
            lambda *refs: flush_kernel(*refs, step=step, chunks=chunks),
            in_specs=[smem, vmem, hbm],
            out_specs=hbm,
            out_shape=like(*out_all.shape),
            scratch_shapes=[pltpu.SemaphoreType.DMA],
            input_output_aliases={2: 0},
            compiler_params=small,
            name="flush",
        )(base, out_piece, out_all)

    def weights(step, g3, g2, g1, after, olds):
        shapes = [(dim, mid), (9 * mid, mid), (mid, dim)]
        return pl.pallas_call(
            lambda *refs: weights_kernel(*refs, step=step, chunks=chunks),
            in_specs=[smem, hbm, hbm, hbm, vmem, vmem, vmem, anywhere] + [vmem] * len(olds),
            out_specs=[vmem] * 3,
            out_shape=[jax.ShapeDtypeStruct(shape, F32) for shape in shapes],
            scratch_shapes=[
                pltpu.VMEM((rows, half, dim), BF16),
                pltpu.VMEM((rows + 2, half, 3 * mid), BF16),
                pltpu.VMEM((rows, half, mid), BF16),
                pltpu.SemaphoreType.DMA((3,)),
            ],
            input_output_aliases={8: 0, 9: 1, 10: 2} if olds else {},
            compiler_params=small,
            name="weights",
        )(base, x_all, pcol, act_two, g3, g2, g1, after, *olds)

    act_a, even, odd, s1 = first(0, 1, None, None)
    even_a, odd_a = exchange(even, odd)
    forward = second(0, 0, act_a, even_a, odd_a, None, None)

    def blank(*shapes):
        return pl.pallas_call(
            lambda *refs: None,
            out_specs=[hbm] * len(shapes),
            out_shape=[like(*shape) for shape in shapes],
            name="blank",
        )()

    out_all, = blank((micros, rows, cols, dim))
    start = jnp.zeros((rows, wide, dim), BF16)
    out_piece = jnp.zeros((rows, half, dim), BF16)
    early, late = {}, {}
    pcol, act_two, s2, d3 = forward
    d_now, s2_now = d3[0], s2[0]
    sums, terms = [], None
    for step in range(steps):
        out_all, g3, g2, even, odd, g3_piece, g2_piece, s1_now = upper(
            step, early.get(step - 2, start), late.get(step - 3)
        )
        even_in, odd_in = exchange(even, odd)
        if terms is not None:
            sums = list(weights(step - 1, *terms, even, sums))
        if step % 2 and (step + 1) // 2 < micros:
            micro = (step + 1) // 2
            forward = second(micro, micro - 1, act_b, even_b, odd_b, forward, sums[2])
            pcol, act_two, s2, d3 = forward
        value, out_piece, g1_piece, d_now, s2_now = lower(
            step, g2, even_in, odd_in, g3, s1_now, sums[2] if sums else even
        )
        terms = (g3_piece, g2_piece, g1_piece)
        if step == 0:
            act_b, even, odd, s1 = first(1, micros, s1, g1_piece)
            even_b, odd_b = exchange(even, odd)
        if step + 2 < steps:
            early[step] = lax.ppermute(value, ("section", "tile"), pairs_down)
        if sections - 2 <= step < sections - 2 + chunks:
            late[step] = lax.ppermute(early[step], ("section", "tile"), pairs_z)
    sums = weights(steps - 1, *terms, g1_piece, sums)
    lines = (dim + 9 * mid + dim) // tiles
    send, keep = pl.pallas_call(
        pack_kernel,
        in_specs=[smem, vmem, vmem, vmem],
        out_specs=[vmem, vmem],
        out_shape=[like(tiles // 2, lines, mid)] * 2,
        compiler_params=small,
        name="pack",
    )(base, *sums)
    came = lax.ppermute(send, "tile", pairs_even)
    both = (keep.astype(F32) + came.astype(F32)).astype(BF16)
    x_size, z_size = 4, 2
    shares = chip_terms(both, x_size, z_size)
    out_all = flush(steps - 1)
    one, two, three = pl.pallas_call(
        finish_kernel,
        in_specs=[vmem] * len(shares),
        out_specs=[vmem] * 3,
        out_shape=[
            jax.ShapeDtypeStruct((dim // tiles, mid), F32),
            jax.ShapeDtypeStruct((9 * mid // tiles, mid), F32),
            jax.ShapeDtypeStruct((mid // tiles, dim), F32),
        ],
        compiler_params=small,
        name="finish",
    )(*shares)
    return (out_all[None], one[None], two[None], three[None])


def solution(mesh):
    return jax.shard_map(
        local,
        mesh=mesh,
        in_specs=(
            P("section", None, "tile", None, None),
            P(None, "tile", None, None),
            P("section", None, None),
            P("section", None, None),
            P("section", None, None),
            P("section", None),
            P("section", None),
            P("section", None),
        ),
        out_specs=(
            P("section", None, "tile", None, None),
            P("section", "tile", None),
            P("section", "tile", None),
            P("section", "tile", None),
        ),
        check_vma=False,
    )
```
